256 devices in a mesh: seq: 32 (over x, y, core), mp: 8 (over z).
Axes of the slice: x: 4, y: 4, z: 8, core: 2. Of those that a mesh axis runs over, the one named last changes fastest.
Arguments:
- hidden: bfloat16 [8192, 8192], P('seq'), may hold values from -6 to 6
- query_weight: bfloat16 [8192, 4096], P('seq', 'mp'), may hold values from -0.0625 to 0.0625
- key_memory: bfloat16 [8192, 4096], P('seq', 'mp'), may hold values from -96 to 96
- value_memory: bfloat16 [8192, 4096], P('seq', 'mp'), may hold values from -6 to 6
- block_len: int32 [64], P('seq'), may hold values from 65 to 128, as said below
- nbr_block: int32 [128, 2], P('seq'), may hold values from 0 to 63, as said below
- out_grad: bfloat16 [8192, 4096], P('seq', 'mp'), may hold values from -6 to 6
Outputs:
- attended: bfloat16 [8192, 4096], P('seq', 'mp')
- d_hidden: bfloat16 [8192, 8192], P(('seq', 'mp'))
- d_key: bfloat16 [8192, 4096], P('seq', 'mp')
- d_value: bfloat16 [8192, 4096], P('seq', 'mp')
The draws below stay inside these ranges and needn't reach their ends.
Inputs may be any that keep to these rules, and one draw needn't show every extreme that they name: `nbr_block`: each retrieval group names two blocks. Block b is held by index b // 2 of seq. The 64-row groups of one index of seq (aligned runs of 4 rows) form 2 * 4 pairs, of which at most one names a block held by any given index of seq; in every draw there is one index of seq whose blocks are named by exactly one pair from every index of seq. `block_len`: some block is full in every draw.
All inputs are finite; a program needn't handle non-finite values.
Results may differ from the reference program's by a relative error of at most 0.035.
Values may be sent and summed in bfloat16 or wider, within the bound.
No kernel may reach another device: no remote copies, remote signals or barrier semaphores. Data moves between devices by JAX's collectives and lax.ppermute only.
A program may use at most 128 MiB of HBM per device.

```python
import jax
import jax.numpy as jnp
from jax import lax

D = 8192
HD = 128
HEADS = 32
GROUP = 64
NLEN = 128
SEQ_LEN = 2048
TOK_DEV = 256
NB_DEV = 2
TOKENS = 8192
NBLK = 64
FEAT = 4096
N_SEQ = 32
N_MP = 8


def draw_key_memory(key, part):
    key = jax.random.fold_in(key, 7)
    base_key = jax.random.fold_in(key, 0)
    row_total = NB_DEV * N_SEQ * NLEN
    base_draw = jnp.clip(jax.random.normal(base_key, (row_total, HEADS * HD), jnp.float32), -6.0, 6.0)
    return base_draw.astype(jnp.bfloat16)


def draw_block_len(key, part):
    key = jax.random.fold_in(key, 5)
    cut_key, keep_key, full_key = jax.random.split(key, 3)
    block_count = NB_DEV * N_SEQ
    cut_rows = jax.random.randint(cut_key, (block_count,), 0, NLEN // 2)
    keep_cut = jax.random.randint(keep_key, (block_count,), 0, 2)
    full_block = jax.random.randint(full_key, (), 0, block_count)
    cut_rows = jnp.where(jnp.arange(block_count, dtype=jnp.int32) == full_block, 0, cut_rows * keep_cut)
    return (NLEN - cut_rows).astype(jnp.int32)


def draw_nbr_block(key, part):
    key = jax.random.fold_in(key, 11)
    tier_key, top_key, noise_key, order_key, pick_key = jax.random.split(key, 5)
    per_device = 2 * TOK_DEV // GROUP
    seat_cap = (per_device + N_SEQ - 1) // N_SEQ
    seat_total = N_SEQ * seat_cap
    seat_index = jnp.arange(seat_total, dtype=jnp.int32)
    owner_tier = jax.random.randint(tier_key, (N_SEQ,), 0, 4)
    top_owner = jax.random.randint(top_key, (), 0, N_SEQ)
    owner_tier = jnp.where(jnp.arange(N_SEQ, dtype=jnp.int32) == top_owner, 12, owner_tier)
    noise_draw = jax.random.randint(noise_key, (N_SEQ, seat_total), 0, 6)
    seat_score = (owner_tier[seat_index // seat_cap][None, :] + noise_draw) * seat_total + seat_index[None, :]
    chosen = lax.top_k(seat_score, per_device)[1]
    mix_score = jax.random.randint(order_key, (N_SEQ, per_device), 0, 1 << 20) * per_device + jnp.arange(per_device, dtype=jnp.int32)[None, :]
    shuffle = jnp.argsort(mix_score, axis=1)
    chosen = jnp.take_along_axis(chosen, shuffle, axis=1)
    owner_of = chosen // seat_cap
    blocks = owner_of * NB_DEV + jax.random.randint(pick_key, (N_SEQ, per_device), 0, NB_DEV)
    return blocks.reshape(N_SEQ * per_device // 2, 2).astype(jnp.int32)


def block_levels(rng, extent, shards, low, top_value):
    def one(position, blocks):
        steps = jax.random.uniform(jax.random.fold_in(jax.random.fold_in(rng, 6), position), (blocks,), jnp.float32, low / len(shards), top_value / len(shards))
        return jnp.repeat(jnp.exp(steps), extent[position] // blocks).reshape((-1,) + (1,) * (len(extent) - position - 1))

    gain = one(*shards[0])
    for cut in shards[1:]:
        gain = gain * one(*cut)
    return gain


def scatter_about(rng, dims, width, most, cuts=(), kind=jnp.bfloat16):
    loudness = block_levels(rng, dims, cuts, -0.22, 0.18) if cuts else 1.0
    drawn = jax.random.normal(rng, dims, jnp.float32) * width * loudness
    return jnp.minimum(jnp.maximum(drawn, -most), most).astype(kind)


def setup_inputs(seed: int = 0) -> dict:
    streams_of = jax.random.split(jax.random.key(seed), 8)
    return {
        "hidden": scatter_about(streams_of[0], (TOKENS, D), 1.0, 6.0, ((0, 32),)),
        "query_weight": scatter_about(streams_of[1], (D, FEAT), D ** -0.5, 0.0625, ((0, 32), (1, 8))),
        "key_memory": draw_key_memory(jax.random.fold_in(streams_of[7], 71), 0),
        "value_memory": scatter_about(streams_of[3], (NBLK * NLEN, FEAT), 1.0, 6.0, ((0, 32), (1, 8))),
        "block_len": draw_block_len(jax.random.fold_in(streams_of[7], 71), 0),
        "nbr_block": draw_nbr_block(jax.random.fold_in(streams_of[7], 71), 0),
        "out_grad": scatter_about(streams_of[6], (TOKENS, FEAT), 1.0, 6.0, ((0, 32), (1, 8))),
    }


NEG_FILL = -1.0e30


def rounded(values):
    return lax.optimization_barrier(values.astype(jnp.bfloat16)).astype(jnp.float32)


def pair_scores(query_rows, key_rows, length):
    row_count, feat_count = query_rows.shape
    head_count = feat_count // HD
    scores = jnp.einsum("qhd,khd->qhk", query_rows.reshape(row_count, head_count, HD).astype(jnp.float32), key_rows.reshape(-1, head_count, HD).astype(jnp.float32)) * (HD ** -0.5)
    valid_keys = (jnp.arange(key_rows.shape[0], dtype=jnp.int32) < length)[None, None, :]
    return jnp.where(valid_keys, scores, NEG_FILL), valid_keys


def pair_forward(query_rows, key_rows, value_rows, length):
    row_count, feat_count = query_rows.shape
    head_count = feat_count // HD
    scores, valid_keys = pair_scores(query_rows, key_rows, length)
    peak_score = jnp.max(scores, axis=2)
    exp_score = jnp.where(valid_keys, jnp.exp(scores - peak_score[..., None]), 0.0)
    exp_total = jnp.sum(exp_score, axis=2)
    partial_value = jnp.einsum("qhk,khd->qhd", rounded(exp_score), value_rows.reshape(-1, head_count, HD).astype(jnp.float32))
    return partial_value, peak_score, exp_total


def pair_backward(query_rows, key_rows, value_rows, length, grad_rows, logsum, row_delta):
    row_count, feat_count = query_rows.shape
    head_count = feat_count // HD
    scores, valid_keys = pair_scores(query_rows, key_rows, length)
    prob_full = jnp.where(valid_keys, jnp.exp(scores - logsum[..., None]), 0.0)
    grad_four = grad_rows.reshape(row_count, head_count, HD).astype(jnp.float32)
    key_four = key_rows.reshape(-1, head_count, HD).astype(jnp.float32)
    value_four = value_rows.reshape(-1, head_count, HD).astype(jnp.float32)
    value_term = jnp.einsum("qhk,qhd->khd", rounded(prob_full), grad_four).astype(jnp.bfloat16)
    grad_prob = jnp.einsum("qhd,khd->qhk", grad_four, value_four)
    dscore = rounded(prob_full * (grad_prob - row_delta[..., None]) * (HD ** -0.5))
    query_term = jnp.einsum("qhk,khd->qhd", dscore, key_four)
    key_term = jnp.einsum("qhk,qhd->khd", dscore, query_rows.reshape(row_count, head_count, HD).astype(jnp.float32)).astype(jnp.bfloat16)
    return query_term.reshape(row_count, feat_count), key_term.reshape(-1, feat_count), value_term.reshape(-1, feat_count)


def reference(hidden, query_weight, key_memory, value_memory, block_len, nbr_block, out_grad):
    tokens = hidden.shape[0]
    feat_count = query_weight.shape[1]
    head_count = feat_count // HD
    rim_rows = GROUP - 1
    group_total = tokens // GROUP
    block_count = block_len.shape[0]
    zero_bf = jnp.zeros((), jnp.bfloat16)
    queries = jnp.dot(hidden, query_weight, preferred_element_type=jnp.float32).astype(jnp.bfloat16)
    positions = jnp.arange(tokens, dtype=jnp.int32)
    live_tok = (positions % SEQ_LEN) >= rim_rows
    live_al = ((positions + rim_rows) % SEQ_LEN) >= rim_rows
    padding = jnp.zeros((rim_rows, feat_count), jnp.bfloat16)
    query_al = jnp.concatenate([queries[rim_rows:], padding], 0)
    grad_al = jnp.where(live_al[:, None], jnp.concatenate([out_grad[rim_rows:], padding], 0), zero_bf)
    key_blocks = key_memory.reshape(block_count, NLEN, feat_count)
    value_blocks = value_memory.reshape(block_count, NLEN, feat_count)

    def group_step(carry_acc, inputs):
        key_acc, value_acc = carry_acc
        query_group, grad_group, pair_blocks = inputs
        pair_parts = []
        for which in range(2):
            block_id = pair_blocks[which].astype(jnp.int32)
            pair_parts.append(pair_forward(query_group, key_blocks[block_id], value_blocks[block_id], block_len[block_id]))
        top_peak = jnp.maximum(pair_parts[0][1], pair_parts[1][1])
        factor_zero = jnp.exp(pair_parts[0][1] - top_peak)
        factor_one = jnp.exp(pair_parts[1][1] - top_peak)
        norm_sum = factor_zero * pair_parts[0][2] + factor_one * pair_parts[1][2]
        mixed_rows = (factor_zero[..., None] * pair_parts[0][0] + factor_one[..., None] * pair_parts[1][0]) / norm_sum[..., None]
        attended_group = mixed_rows.astype(jnp.bfloat16).reshape(GROUP, feat_count)
        logsum = top_peak + jnp.log(norm_sum)
        row_delta = jnp.sum((grad_group.astype(jnp.float32) * attended_group.astype(jnp.float32)).reshape(GROUP, head_count, HD), axis=2)
        grad_query = jnp.zeros((GROUP, feat_count), jnp.float32)
        for which in range(2):
            block_id = pair_blocks[which].astype(jnp.int32)
            query_term, key_term, value_term = pair_backward(query_group, key_blocks[block_id], value_blocks[block_id], block_len[block_id], grad_group, logsum, row_delta)
            grad_query = grad_query + query_term
            key_acc = key_acc.at[block_id].add(key_term.astype(jnp.float32))
            value_acc = value_acc.at[block_id].add(value_term.astype(jnp.float32))
        return (key_acc, value_acc), (attended_group, grad_query.astype(jnp.bfloat16))

    start_acc = (jnp.zeros((block_count, NLEN, feat_count), jnp.float32), jnp.zeros((block_count, NLEN, feat_count), jnp.float32))
    (key_acc, value_acc), (attended_groups, grad_groups) = lax.scan(group_step, start_acc, (query_al.reshape(group_total, GROUP, feat_count), grad_al.reshape(group_total, GROUP, feat_count), nbr_block.astype(jnp.int32)))
    attended_al = attended_groups.reshape(tokens, feat_count)
    grad_query_al = grad_groups.reshape(tokens, feat_count)
    attended = jnp.where(live_tok[:, None], jnp.concatenate([padding, attended_al[:tokens - rim_rows]], 0), zero_bf)
    query_grad = jnp.where(live_tok[:, None], jnp.concatenate([padding, grad_query_al[:tokens - rim_rows]], 0), zero_bf)
    group_width = feat_count // N_MP
    d_hidden = jnp.zeros((tokens, hidden.shape[1]), jnp.float32)
    for group_idx in range(N_MP):
        term_rows = jnp.dot(query_grad[:, group_idx * group_width:(group_idx + 1) * group_width], query_weight[:, group_idx * group_width:(group_idx + 1) * group_width].T, preferred_element_type=jnp.float32)
        d_hidden = d_hidden + rounded(term_rows)
    d_key = key_acc.astype(jnp.bfloat16).reshape(block_count * NLEN, feat_count)
    d_value = value_acc.astype(jnp.bfloat16).reshape(block_count * NLEN, feat_count)
    return attended, d_hidden.astype(jnp.bfloat16), d_key, d_value
```

```python
import functools

import jax
import jax.numpy as jnp
from jax import lax
from jax.experimental import pallas as pl
from jax.experimental.pallas import tpu as pltpu
from jax.sharding import PartitionSpec as P

HD = 128
GROUP = 64
NLEN = 128
SEQ_LEN = 2048
RIM = GROUP - 1
NX, NY, NC = 4, 4, 2
NS = NX * NY * NC
NM = 8
TOK = 256
FT = 512
DM = 8192
HALF = FT // 2
NH = FT // HD
NP = 8
NB = 64
RQ = 4
QR = NLEN // RQ
BF = jnp.bfloat16
F32 = jnp.float32
NEG_FILL = -1e30
MIB = 1 << 20


def hop(v, dx=0, dy=0, dc=0):
    pairs = []
    for x in range(NX):
        for y in range(NY):
            for c in range(NC):
                to = (((x + dx) % NX) * NY + (y + dy) % NY) * NC + (c ^ dc)
                pairs.append(((x * NY + y) * NC + c, to))
    return lax.ppermute(v, "seq", pairs)


def to_seq(v, by):
    return lax.ppermute(v, "seq", [(i, (i + by) % NS) for i in range(NS)])


def ring4(v, axis):
    def go(u, d):
        return hop(u, dx=d) if axis == 0 else hop(u, dy=d)

    low, high = go(v, 1), go(v, -1)
    half = v.shape[0] // 2
    far = jnp.concatenate([go(low[:half], 1), go(high[half:], -1)], 0)
    return low, far, high


OFF = (0, -1, -2, 1)


def gather_weight(w):
    left, right = w[:, :HALF], w[:, HALF:]
    a1 = jnp.concatenate((left,) + ring4(left, 0), 0).reshape(4, 256, HALF)
    b1 = jnp.concatenate((right,) + ring4(right, 1), 0).reshape(4, 256, HALF)
    a2 = jnp.concatenate((a1,) + ring4(a1, 1), 0)
    b2 = jnp.concatenate((b1,) + ring4(b1, 0), 0)
    return a2, b2, hop(a2, dc=1), hop(b2, dc=1)


def query_kernel(chip, core, hid, ao, asb, bo, bsb, out, acc):
    k = pl.program_id(0)

    @pl.when(k == 0)
    def _():
        acc[...] = jnp.zeros_like(acc)

    c = core[0]
    ho = hid[:, pl.ds(pl.multiple_of(c * 256, 256), 256)]
    hs = hid[:, pl.ds(pl.multiple_of((1 - c) * 256, 256), 256)]

    def dot(p, r):
        return jnp.dot(p, r, preferred_element_type=F32)

    acc[:, :HALF] += dot(ho, ao[0]) + dot(hs, asb[0])
    acc[:, HALF:] += dot(ho, bo[0]) + dot(hs, bsb[0])

    @pl.when(k == pl.num_programs(0) - 1)
    def _():
        out[...] = acc[...].astype(BF)


def weight_specs():
    first = pl.BlockSpec((1, 256, HALF), lambda k, *_: (k, 0, 0))
    second = pl.BlockSpec((1, 256, HALF), lambda k, *_: ((k % 4) * 4 + k // 4, 0, 0))
    return [first, first, second, second]


def project(hidden, chips, core, ao, asb, bo, bsb):
    return pl.pallas_call(
        query_kernel,
        out_shape=jax.ShapeDtypeStruct((TOK, FT), BF),
        grid_spec=pltpu.PrefetchScalarGridSpec(
            num_scalar_prefetch=2,
            grid=(NX * NY,),
            in_specs=[pl.BlockSpec((TOK, 512), lambda k, chip, core: (0, chip[k]))] + weight_specs(),
            out_specs=pl.BlockSpec((TOK, FT), lambda k, *_: (0, 0)),
            scratch_shapes=[pltpu.VMEM((TOK, FT), F32)],
        ),
        compiler_params=pltpu.CompilerParams(vmem_limit_bytes=16 * MIB),
        cost_estimate=pl.CostEstimate(flops=2 * TOK * DM * FT, bytes_accessed=12 * MIB, transcendentals=0),
    )(chips, core, hidden, ao, asb, bo, bsb)


def pick_kernel(ids, table, out):
    def step(p, _):
        out[p] = table[ids[p]]
        return 0

    lax.fori_loop(0, NS * NP, step, 0, unroll=8)


def pick(ids, table):
    return pl.pallas_call(
        pick_kernel,
        out_shape=jax.ShapeDtypeStruct((NS * NP, QR, HD), BF),
        in_specs=[pl.BlockSpec(memory_space=pltpu.SMEM), pl.BlockSpec(memory_space=pltpu.VMEM)],
        out_specs=pl.BlockSpec(memory_space=pltpu.VMEM),
        compiler_params=pltpu.CompilerParams(vmem_limit_bytes=16 * MIB),
    )(ids, table)


def total_kernel(ids, terms, out, acc):
    acc[...] = jnp.zeros_like(acc)

    def step(p, _):
        b = ids[p]
        acc[b] = acc[b] + terms[p].astype(F32)
        return 0

    lax.fori_loop(0, NS * NP, step, 0, unroll=4)
    out[...] = acc[...].astype(BF)


def total(ids, terms):
    return pl.pallas_call(
        total_kernel,
        out_shape=jax.ShapeDtypeStruct((NB, QR, HD), BF),
        in_specs=[pl.BlockSpec(memory_space=pltpu.SMEM), pl.BlockSpec(memory_space=pltpu.VMEM)],
        out_specs=pl.BlockSpec(memory_space=pltpu.VMEM),
        scratch_shapes=[pltpu.VMEM((NB, QR, HD), F32)],
        compiler_params=pltpu.CompilerParams(vmem_limit_bytes=16 * MIB),
    )(ids, terms)


def attend_kernel(mine, lens, last, q, qn, g, gn, kv, att, gq, terms):
    def mm(p, r, dims):
        return lax.dot_general(p, r, (dims, ((), ())), preferred_element_type=F32)

    row = lax.broadcasted_iota(jnp.int32, (TOK, TOK + GROUP), 0)
    col = lax.broadcasted_iota(jnp.int32, (TOK, TOK + GROUP), 1)
    shift = (col == row + RIM).astype(F32).astype(BF)
    q_ext = jnp.concatenate([q[...], qn[...]], 0)
    g_next = gn[...]
    g_next = jnp.where(last[0] == 1, jnp.zeros_like(g_next), g_next)
    g_ext = jnp.concatenate([g[...], g_next], 0)
    q_al = mm(shift, q_ext, ((1,), (0,))).astype(BF)
    g_al = mm(shift, g_ext, ((1,), (0,))).astype(BF)
    scale = HD ** (-0.5)
    lane = lax.broadcasted_iota(jnp.int32, (GROUP, 2 * NLEN), 1)
    for grp in range(TOK // GROUP):
        rows = slice(grp * GROUP, (grp + 1) * GROUP)
        qg, gg = q_al[rows], g_al[rows]
        keys = jnp.concatenate([kv[0, 0, r, 2 * grp + n] for n in range(2) for r in range(RQ)], 0)
        vals = jnp.concatenate([kv[1, 0, r, 2 * grp + n] for n in range(2) for r in range(RQ)], 0)
        len0 = lens[mine[2 * grp]]
        len1 = lens[mine[2 * grp + 1]]
        valid = lane < jnp.where(lane < NLEN, len0, len1 + NLEN)
        scores = jnp.where(valid, mm(qg, keys, ((1,), (1,))) * scale, NEG_FILL)
        top = jnp.max(scores, axis=1, keepdims=True)
        ex = jnp.where(valid, jnp.exp(scores - top), 0.0)
        norm = jnp.sum(ex, axis=1, keepdims=True)
        inv = 1.0 / norm
        out = (mm(ex.astype(BF), vals, ((1,), (0,))) * inv).astype(BF)
        att[rows, :] = out
        delta = jnp.sum(gg.astype(F32) * out.astype(F32), axis=1, keepdims=True)
        prob = ex * inv
        grad_prob = mm(gg, vals, ((1,), (1,)))
        ds = (prob * (grad_prob - delta) * scale).astype(BF)
        gq[rows, :] = mm(ds, keys, ((1,), (0,))).astype(BF)
        vt = mm(prob.astype(BF), gg, ((0,), (0,))).astype(BF)
        kt = mm(ds, qg, ((0,), (0,))).astype(BF)
        for n in range(2):
            for r in range(RQ):
                part = slice((n * RQ + r) * QR, (n * RQ + r + 1) * QR)
                terms[0, 0, r, 2 * grp + n] = kt[part]
                terms[1, 0, r, 2 * grp + n] = vt[part]


def attend(mine, lens, last, q, qn, g, gn, kv):
    tok = pl.BlockSpec((TOK, HD), lambda h, *_: (0, h))
    rim = pl.BlockSpec((GROUP, HD), lambda h, *_: (0, h))
    mem = pl.BlockSpec((2, 1, RQ, NP, QR, HD), lambda h, *_: (0, h, 0, 0, 0, 0))
    rows = jax.ShapeDtypeStruct((TOK, FT), BF)
    return pl.pallas_call(
        attend_kernel,
        out_shape=(rows, rows, jax.ShapeDtypeStruct((2, NH, RQ, NP, QR, HD), BF)),
        grid_spec=pltpu.PrefetchScalarGridSpec(
            num_scalar_prefetch=3,
            grid=(NH,),
            in_specs=[tok, rim, tok, rim, mem],
            out_specs=(tok, tok, mem),
        ),
        compiler_params=pltpu.CompilerParams(vmem_limit_bytes=24 * MIB),
        cost_estimate=pl.CostEstimate(flops=400_000_000, bytes_accessed=6 * MIB, transcendentals=TOK * NLEN * 2 * NH),
    )(mine, lens, last, q, qn, g, gn, kv)


def hidden_kernel(lo, chip, order, core, gq, tail, ao, asb, bo, bsb, out, rows):
    count = rows.shape[0]
    k = pl.program_id(0)

    def mm(p, r, dims):
        return lax.dot_general(p, r, (dims, ((), ())), preferred_element_type=F32)

    @pl.when(k == 0)
    def _():
        ext = jnp.concatenate([gq[...], tail[...]], 0)
        base = lax.broadcasted_iota(jnp.int32, (32, TOK + GROUP), 0)
        col = lax.broadcasted_iota(jnp.int32, (32, TOK + GROUP), 1)
        first = order[NM]
        for part in range(count // 32):
            tok = base + order[lo + part] * 32
            src = jnp.where(tok < RIM, jnp.where(first == 1, -1, tok + (TOK + 1)), tok - RIM)
            pickm = (col == src).astype(F32).astype(BF)
            rows[part * 32 : (part + 1) * 32, :] = mm(pickm, ext, ((1,), (0,))).astype(BF)

    c = core[0]
    own = mm(rows[:, :HALF], ao[0], ((1,), (1,))) + mm(rows[:, HALF:], bo[0], ((1,), (1,)))
    sib = mm(rows[:, :HALF], asb[0], ((1,), (1,))) + mm(rows[:, HALF:], bsb[0], ((1,), (1,)))
    out[:, pl.ds(pl.multiple_of(c * 256, 256), 256)] = own.astype(BF)
    out[:, pl.ds(pl.multiple_of((1 - c) * 256, 256), 256)] = sib.astype(BF)


def hidden_part(lo, count, chips, order, core, gq, tail, ao, asb, bo, bsb):
    return pl.pallas_call(
        functools.partial(hidden_kernel, lo),
        out_shape=jax.ShapeDtypeStruct((count * 32, DM), BF),
        grid_spec=pltpu.PrefetchScalarGridSpec(
            num_scalar_prefetch=3,
            grid=(NX * NY,),
            in_specs=[
                pl.BlockSpec((TOK, FT), lambda k, *_: (0, 0)),
                pl.BlockSpec((GROUP, FT), lambda k, *_: (0, 0)),
            ]
            + weight_specs(),
            out_specs=pl.BlockSpec((count * 32, 512), lambda k, chip, *_: (0, chip[k])),
            scratch_shapes=[pltpu.VMEM((count * 32, FT), BF)],
        ),
        compiler_params=pltpu.CompilerParams(vmem_limit_bytes=16 * MIB),
        cost_estimate=pl.CostEstimate(flops=2 * 32 * count * DM * FT, bytes_accessed=12 * MIB, transcendentals=0),
    )(chips, order, core, gq, tail, ao, asb, bo, bsb)


def ring_pairs():
    pairs = []
    for s in range(NS):
        step = 1 if s % 2 == 0 else -1
        for m in range(NM):
            pairs.append((s * NM + m, s * NM + (m + step) % NM))
    return pairs


def around(v):
    return lax.ppermute(v, ("seq", "mp"), ring_pairs())


def swap_all(v):
    return lax.all_to_all(v, "seq", split_axis=0, concat_axis=0, tiled=True)


def shards(hidden, query_weight, key_memory, value_memory, block_len, nbr_block, out_grad):
    s = lax.axis_index("seq")
    m = lax.axis_index("mp")
    core = s % NC
    cx, cy = s // (NY * NC), (s // NC) % NY
    off = jnp.array(OFF, jnp.int32)
    chips = (((cx + off[None, :]) % NX) * NY + (cy + off[:, None]) % NY).reshape(-1).astype(jnp.int32)
    core1 = core.reshape(1).astype(jnp.int32)
    last = (s % 8 == 7).astype(jnp.int32).reshape(1)
    first = (s % 8 == 0).astype(jnp.int32).reshape(1)
    way = 1 - 2 * core
    order = (m - way * (1 + jnp.arange(NM, dtype=jnp.int32))) % NM
    order = jnp.concatenate([order, first]).astype(jnp.int32)
    mine = nbr_block.reshape(NP)

    def sliced(v):
        return v.reshape(2, RQ, QR, NH, HD).transpose(3, 1, 0, 2, 4).reshape(NH * RQ, 2 * QR, HD)

    meta = jnp.concatenate([mine, block_len]).astype(BF)
    meta = jnp.broadcast_to(jnp.pad(meta, (0, HD - NP - 2))[None, None, :], (NS, 16, HD))
    pay = jnp.concatenate([jnp.concatenate([sliced(key_memory), sliced(value_memory)], 0), meta], 1)
    held = swap_all(pay)
    table = held[:, : 2 * QR].reshape(NB, QR, HD)
    facts = held[:, 2 * QR, : NP + 2].astype(jnp.int32)
    ids = facts[:, :NP].reshape(NS * NP)
    lens = facts[:, NP:].reshape(NB)
    sent = pick(ids, table).reshape(NS, NP * QR, HD)
    kv = swap_all(sent).reshape(2, NH, RQ, NP, QR, HD)

    ao, bo, asb, bsb = gather_weight(query_weight)
    g_next = to_seq(out_grad[:GROUP], -1)
    queries = project(hidden, chips, core1, ao, asb, bo, bsb)
    q_next = to_seq(queries[:GROUP], -1)

    att_al, gq_al, terms = attend(mine, lens, last, queries, q_next, out_grad, g_next, kv)
    gq_tail = to_seq(gq_al[TOK - GROUP :], 1)
    att_tail = to_seq(att_al[TOK - GROUP :], 1)

    def part(lo, count):
        return hidden_part(lo, count, chips, order, core1, gq_al, gq_tail, ao, asb, bo, bsb)

    run = part(0, 1)
    rest = part(1, NM - 1)
    for k in range(NM - 1):
        run = around(run)
        run = (run.astype(F32) + rest[k * 32 : (k + 1) * 32].astype(F32)).astype(BF)

    got = swap_all(terms.reshape(NS, NP * QR, HD)).reshape(NS * NP, QR, HD)
    sums = total(ids, got).reshape(NS, 2 * QR, HD)
    back = swap_all(sums).reshape(2, NH, RQ, 2, QR, HD)
    grads = back.transpose(0, 3, 2, 4, 1, 5).reshape(2, 2 * NLEN, FT)

    dead = jnp.where(first[0] == 1, jnp.zeros((), BF), att_tail[1:])
    attended = jnp.concatenate([dead, att_al[: TOK - RIM]], 0)
    return attended, run, grads[0], grads[1]


def solution(mesh):
    return jax.shard_map(
        shards,
        mesh=mesh,
        in_specs=(
            P("seq", None),
            P("seq", "mp"),
            P("seq", "mp"),
            P("seq", "mp"),
            P("seq"),
            P("seq", None),
            P("seq", "mp"),
        ),
        out_specs=(P("seq", "mp"), P(("seq", "mp"), None), P("seq", "mp"), P("seq", "mp")),
        check_vma=False,
    )
```

```python
import functools

import jax
import jax.numpy as jnp
from jax import lax
from jax.experimental import pallas as pl
from jax.experimental.pallas import tpu as pltpu
from jax.sharding import PartitionSpec as P

HD = 128
GROUP = 64
NLEN = 128
SEQ_LEN = 2048
RIM = GROUP - 1
NX, NY, NC = 4, 4, 2
NS = NX * NY * NC
NM = 8
TOK = 256
FT = 512
DM = 8192
HALF = FT // 2
NH = FT // HD
NP = 8
NB = 64
RQ = 4
QR = NLEN // RQ
BF = jnp.bfloat16
F32 = jnp.float32
NEG_FILL = -1e30
MIB = 1 << 20
WIDE = 56 * MIB


def hop(v, dx=0, dy=0, dc=0):
    pairs = []
    for x in range(NX):
        for y in range(NY):
            for c in range(NC):
                to = (((x + dx) % NX) * NY + (y + dy) % NY) * NC + (c ^ dc)
                pairs.append(((x * NY + y) * NC + c, to))
    return lax.ppermute(v, "seq", pairs)


def to_seq(v, by):
    return lax.ppermute(v, "seq", [(i, (i + by) % NS) for i in range(NS)])


def along(v, axis, by):
    return hop(v, dx=by) if axis == 0 else hop(v, dy=by)


OFF = (0, -1, -2, 1)


def near(v, axis):
    return along(v, axis, 1), along(v, axis, 2), along(v, axis, -1)


def prepare_kernel(mine, lens, key, value, w, g, pay, left, right, g_head):
    lane = lax.broadcasted_iota(jnp.int32, (16, HD), 1)
    meta = jnp.zeros((16, HD), jnp.int32)
    for i in range(NP):
        meta = jnp.where(lane == i, mine[i % 2, i // 2], meta)
    for i in range(2):
        meta = jnp.where(lane == NP + i, lens[i], meta)
    meta = meta.astype(F32).astype(BF)
    for which, ref in ((0, key), (1, value)):
        for h in range(NH):
            for r in range(RQ):
                j = (which * NH + h) * RQ + r
                for blk in range(2):
                    at = blk * NLEN + r * QR
                    pay[j, blk * QR : (blk + 1) * QR] = ref[at : at + QR, h * HD : (h + 1) * HD]
                pay[j, 2 * QR :] = meta
    left[...] = w[:, :HALF]
    right[...] = w[:, HALF:]
    g_head[...] = g[...]


def prepare(mine, lens, key, value, w, g):
    smem = pl.BlockSpec(memory_space=pltpu.SMEM)

    def full(*shape):
        return pl.BlockSpec(shape, lambda i: (0,) * len(shape))

    half = jax.ShapeDtypeStruct((256, HALF), BF)
    return pl.pallas_call(
        prepare_kernel,
        grid=(1,),
        out_shape=(
            jax.ShapeDtypeStruct((NS, 2 * QR + 16, HD), BF),
            half,
            half,
            jax.ShapeDtypeStruct((GROUP, FT), BF),
        ),
        in_specs=[smem, smem, full(256, FT), full(256, FT), full(256, FT), full(GROUP, FT)],
        out_specs=(full(NS, 2 * QR + 16, HD), full(256, HALF), full(256, HALF), full(GROUP, FT)),
        compiler_params=pltpu.CompilerParams(vmem_limit_bytes=WIDE),
    )(mine, lens, key, value, w, g)


def stack_kernel(*refs):
    a, b, oa, ob = refs[:4], refs[4:8], refs[8], refs[9]
    for i in range(4):
        oa[i] = a[i][...]
        ob[i] = b[i][...]


def stack(a, b):
    shape = jax.ShapeDtypeStruct((4, 256, HALF), BF)
    return pl.pallas_call(
        stack_kernel,
        out_shape=(shape, shape),
        compiler_params=pltpu.CompilerParams(vmem_limit_bytes=16 * MIB),
        cost_estimate=pl.CostEstimate(flops=0, bytes_accessed=2 * MIB, transcendentals=0),
    )(*a, *b)


def block_of(pieces, i, j):
    own, low, f0, f1, high = pieces
    if i == 0:
        return own[j]
    if i == 1:
        return low[j]
    if i == 2:
        return f0[j] if j < 2 else f1[j - 2]
    return high[j]


def join_kernel(*refs):
    a, b, out = refs[:5], refs[5:10], refs[10]
    for dy in range(4):
        for dx in range(4):
            out[dy * 4 + dx, :HALF] = block_of(a, dy, dx).T
            out[dy * 4 + dx, HALF:] = block_of(b, dx, dy).T


def join(a, b):
    return pl.pallas_call(
        join_kernel,
        out_shape=jax.ShapeDtypeStruct((NX * NY, FT, 256), BF),
        compiler_params=pltpu.CompilerParams(vmem_limit_bytes=WIDE),
        cost_estimate=pl.CostEstimate(flops=0, bytes_accessed=1024, transcendentals=0),
    )(*a, *b)


def query_kernel(chip, core, hid, hsib, *refs):
    a, b = refs[:5], refs[5:10]
    own, sib, own_head, sib_head, cols, acc, sems = refs[10:]
    c = core[0]

    def copies(k):
        src = pl.ds(pl.multiple_of(chip[k] * 512 + c * 256, 256), 256)
        dst = pl.ds(k * 256, 256)
        return (
            pltpu.make_async_copy(hid.at[:, src], cols.at[pl.ds(0, TOK), dst], sems.at[0, k]),
            pltpu.make_async_copy(hsib.at[:, src], cols.at[pl.ds(TOK, TOK), dst], sems.at[1, k]),
        )

    for k in range(16):
        for cp in copies(k):
            cp.start()
    for dy in range(4):
        for k in range(4 * dy, 4 * dy + 4):
            for cp in copies(k):
                cp.wait()
        left = jnp.concatenate([block_of(a, dy, dx) for dx in range(4)], 0)
        right = jnp.concatenate([block_of(b, dx, dy) for dx in range(4)], 0)
        h = cols[:, dy * 1024 : (dy + 1) * 1024]
        for n, w in ((0, left), (1, right)):
            part = jnp.dot(h, w, preferred_element_type=F32)
            if dy:
                part = part + acc[:, n * HALF : (n + 1) * HALF]
            acc[:, n * HALF : (n + 1) * HALF] = part
    own[...] = acc[:TOK]
    sib[...] = acc[TOK:]
    own_head[...] = acc[:GROUP]
    sib_head[...] = acc[TOK : TOK + GROUP]


def project(hidden, hsib, chips, core, a, b):
    whole = jax.ShapeDtypeStruct((TOK, FT), F32)
    head = jax.ShapeDtypeStruct((GROUP, FT), F32)
    smem = pl.BlockSpec(memory_space=pltpu.SMEM)
    hbm = pl.BlockSpec(memory_space=pl.ANY)
    vmem = pl.BlockSpec(memory_space=pltpu.VMEM)
    return pl.pallas_call(
        query_kernel,
        out_shape=(whole, whole, head, head),
        in_specs=[smem, smem, hbm, hbm] + [vmem] * 10,
        out_specs=(vmem,) * 4,
        scratch_shapes=[
            pltpu.VMEM((2 * TOK, DM // 2), BF),
            pltpu.VMEM((2 * TOK, FT), F32),
            pltpu.SemaphoreType.DMA((2, 16)),
        ],
        compiler_params=pltpu.CompilerParams(vmem_limit_bytes=WIDE),
        cost_estimate=pl.CostEstimate(flops=0, bytes_accessed=1024, transcendentals=0),
    )(chips, core, hidden, hsib, *a, *b)


def pick_kernel(facts, held, out):
    count = out.shape[0] // NP
    base = pl.program_id(0) * count

    def step(i, _):
        for n in range(NP):
            b = facts[base + i, n]
            at = pl.multiple_of(jnp.bitwise_and(b, 1) * QR, QR)
            out[i * NP + n] = held[lax.shift_right_logical(b, 1), pl.ds(at, QR)]
        return 0

    lax.fori_loop(0, count, step, 0, unroll=2)


def pick(facts, held):
    count = NS * NP // 2
    return pl.pallas_call(
        pick_kernel,
        out_shape=jax.ShapeDtypeStruct((NS * NP, QR, HD), BF),
        grid=(2,),
        in_specs=[pl.BlockSpec(memory_space=pltpu.SMEM), pl.BlockSpec(held.shape, lambda i: (0, 0, 0))],
        out_specs=pl.BlockSpec((count, QR, HD), lambda i: (i, 0, 0)),
        compiler_params=pltpu.CompilerParams(vmem_limit_bytes=WIDE),
        cost_estimate=pl.CostEstimate(flops=0, bytes_accessed=1024, transcendentals=0),
    )(facts, held)


def total_kernel(facts, terms, out, acc):
    acc[...] = jnp.zeros_like(acc)

    def step(i, _):
        for n in range(NP):
            b = facts[i, n]
            acc[b] = acc[b] + terms[i * NP + n].astype(F32)
        return 0

    lax.fori_loop(0, NS, step, 0, unroll=2)
    out[...] = acc[...].astype(BF)


def total(facts, terms):
    return pl.pallas_call(
        total_kernel,
        out_shape=jax.ShapeDtypeStruct((NB, QR, HD), BF),
        in_specs=[pl.BlockSpec(memory_space=pltpu.SMEM), pl.BlockSpec(memory_space=pltpu.VMEM)],
        out_specs=pl.BlockSpec(memory_space=pltpu.VMEM),
        scratch_shapes=[pltpu.VMEM((NB, QR, HD), F32)],
        compiler_params=pltpu.CompilerParams(vmem_limit_bytes=16 * MIB),
    )(facts, terms)


def attend_kernel(groups, mine, facts, last, qa, qb, na, nb, g, gn, kv, *rest):
    att, gq, terms = rest[-3:]

    def mm(p, r, dims):
        return lax.dot_general(p, r, (dims, ((), ())), preferred_element_type=F32)

    count = len(groups) * GROUP
    lo = groups[0] * GROUP
    ext = min(count + GROUP, TOK - lo)
    row = lax.broadcasted_iota(jnp.int32, (count, ext + GROUP), 0)
    col = lax.broadcasted_iota(jnp.int32, (count, ext + GROUP), 1)
    shift = (col == row + RIM).astype(F32).astype(BF)
    q_next = (na[...] + nb[...]).astype(BF)
    g_next = gn[...]
    g_next = jnp.where(last[0] == 1, jnp.zeros_like(g_next), g_next)
    q_ext = jnp.concatenate([(qa[lo : lo + ext] + qb[lo : lo + ext]).astype(BF), q_next], 0)
    g_ext = jnp.concatenate([g[lo : lo + ext], g_next], 0)
    q_al = mm(shift, q_ext, ((1,), (0,))).astype(BF)
    g_al = mm(shift, g_ext, ((1,), (0,))).astype(BF)
    scale = HD ** (-0.5)
    lane = lax.broadcasted_iota(jnp.int32, (GROUP, 2 * NLEN), 1)
    for i, grp in enumerate(groups):
        rows = slice(i * GROUP, (i + 1) * GROUP)
        qg, gg = q_al[rows], g_al[rows]
        keys = jnp.concatenate([kv[0, 0, r, 2 * i + n] for n in range(2) for r in range(RQ)], 0)
        vals = jnp.concatenate([kv[1, 0, r, 2 * i + n] for n in range(2) for r in range(RQ)], 0)
        blk0, blk1 = mine[0, grp], mine[1, grp]
        len0 = facts[lax.shift_right_logical(blk0, 1), NP + jnp.bitwise_and(blk0, 1)]
        len1 = facts[lax.shift_right_logical(blk1, 1), NP + jnp.bitwise_and(blk1, 1)]
        valid = lane < jnp.where(lane < NLEN, len0, len1 + NLEN)
        scores = jnp.where(valid, mm(qg, keys, ((1,), (1,))) * scale, NEG_FILL)
        top = jnp.max(scores, axis=1, keepdims=True)
        ex = jnp.where(valid, jnp.exp(scores - top), 0.0)
        norm = jnp.sum(ex, axis=1, keepdims=True)
        inv = 1.0 / norm
        out = (mm(ex.astype(BF), vals, ((1,), (0,))) * inv).astype(BF)
        att[rows, :] = out
        delta = jnp.sum(gg.astype(F32) * out.astype(F32), axis=1, keepdims=True)
        prob = ex * inv
        grad_prob = mm(gg, vals, ((1,), (1,)))
        ds = (prob * (grad_prob - delta) * scale).astype(BF)
        gq[rows, :] = mm(ds, keys, ((1,), (0,))).astype(BF)
        vt = mm(prob.astype(BF), gg, ((0,), (0,))).astype(BF)
        kt = mm(ds, qg, ((0,), (0,))).astype(BF)
        for n in range(2):
            for r in range(RQ):
                part = slice((n * RQ + r) * QR, (n * RQ + r + 1) * QR)
                terms[0, 0, r, 2 * i + n] = kt[part]
                terms[1, 0, r, 2 * i + n] = vt[part]


def attend(groups, mine, facts, last, qa, qb, na, nb, g, gn, kv, into=None):
    count = len(groups) * GROUP
    place = groups[0] // len(groups)
    tok = pl.BlockSpec((TOK, HD), lambda h, *_: (0, h))
    rim = pl.BlockSpec((GROUP, HD), lambda h, *_: (0, h))
    out = pl.BlockSpec((count, HD), lambda h, *_: (0, h))
    mem = pl.BlockSpec((2, 1, RQ, 2 * len(groups), QR, HD), lambda h, *_: (0, h, 0, place, 0, 0))
    rows = jax.ShapeDtypeStruct((count, FT), BF)
    specs, operands, alias = [tok, tok, rim, rim, tok, rim, mem], (qa, qb, na, nb, g, gn, kv), {}
    if into is not None:
        specs, operands, alias = specs + [pl.BlockSpec(memory_space=pl.ANY)], operands + (into,), {10: 2}
    return pl.pallas_call(
        functools.partial(attend_kernel, groups),
        out_shape=(rows, rows, jax.ShapeDtypeStruct((2, NH, RQ, NP, QR, HD), BF)),
        grid_spec=pltpu.PrefetchScalarGridSpec(
            num_scalar_prefetch=3,
            grid=(NH,),
            in_specs=specs,
            out_specs=(out, out, mem),
        ),
        input_output_aliases=alias,
        compiler_params=pltpu.CompilerParams(vmem_limit_bytes=WIDE),
        cost_estimate=pl.CostEstimate(
            flops=100_000_000 * len(groups), bytes_accessed=2 * MIB * len(groups), transcendentals=0
        ),
    )(mine, facts, last, *operands)


def hidden_kernel(lo, chip, order, core, gq, end, tail, wo, ws, left, right, *more):
    rows = more[-1]
    count = rows.shape[0] // 32
    k = pl.program_id(0)

    def mm(p, r):
        return jnp.dot(p, r, preferred_element_type=F32)

    @pl.when(k == 0)
    def _():
        ext = jnp.concatenate([gq[...], end[...], tail[...]], 0)
        base = lax.broadcasted_iota(jnp.int32, (32, TOK + GROUP), 0)
        col = lax.broadcasted_iota(jnp.int32, (32, TOK + GROUP), 1)
        first = order[NM]
        for part in range(count):
            tok = base + order[lo + part] * 32
            src = jnp.where(tok < RIM, jnp.where(first == 1, -1, tok + (TOK + 1)), tok - RIM)
            pickm = (col == src).astype(F32).astype(BF)
            rows[part * 32 : (part + 1) * 32, :] = mm(pickm, ext).astype(BF)

    c = core[0]
    for dx in range(4):
        place = chip[k * 4 + dx]
        half = place // 8
        own = mm(rows[...], wo[dx]).astype(BF)
        sib = mm(rows[...], ws[dx]).astype(BF)
        at = (place - 8 * half) * 512
        own_at = pl.ds(pl.multiple_of(at + c * 256, 256), 256)
        sib_at = pl.ds(pl.multiple_of(at + (1 - c) * 256, 256), 256)

        @pl.when(half == 0)
        def _():
            left[:, own_at] = own
            left[:, sib_at] = sib
            if count > 1:
                more[0][:, own_at] = own[32:64]
                more[0][:, sib_at] = sib[32:64]

        @pl.when(half == 1)
        def _():
            right[:, own_at] = own
            right[:, sib_at] = sib
            if count > 1:
                more[1][:, own_at] = own[:32]
                more[1][:, sib_at] = sib[:32]


def hidden_part(lo, count, chips, order, core, gq, end, tail, wo, ws):
    shape = jax.ShapeDtypeStruct((count * 32, DM // 2), BF)
    half = pl.BlockSpec((count * 32, DM // 2), lambda k, *_: (0, 0))
    shapes, halves = (shape, shape), (half, half)
    if count > 1:
        shapes += (jax.ShapeDtypeStruct((32, DM // 2), BF),) * 2
        halves += (pl.BlockSpec((32, DM // 2), lambda k, *_: (0, 0)),) * 2
    weight = pl.BlockSpec((4, FT, 256), lambda k, *_: (k, 0, 0))
    return pl.pallas_call(
        functools.partial(hidden_kernel, lo),
        out_shape=shapes,
        grid_spec=pltpu.PrefetchScalarGridSpec(
            num_scalar_prefetch=3,
            grid=(4,),
            in_specs=[
                pl.BlockSpec((TOK - GROUP, FT), lambda k, *_: (0, 0)),
                pl.BlockSpec((GROUP, FT), lambda k, *_: (0, 0)),
                pl.BlockSpec((GROUP, FT), lambda k, *_: (0, 0)),
                weight,
                weight,
            ],
            out_specs=halves,
            scratch_shapes=[pltpu.VMEM((count * 32, FT), BF)],
        ),
        compiler_params=pltpu.CompilerParams(vmem_limit_bytes=24 * MIB),
        cost_estimate=pl.CostEstimate(
            flops=0 if count > 1 else 8 * TOK * DM * FT, bytes_accessed=1024 if count > 1 else 60 * MIB, transcendentals=0
        ),
    )(chips, order, core, gq, end, tail, wo, ws)


def around(v, by):
    return lax.ppermute(v, "mp", [(i, (i + by) % NM) for i in range(NM)])


def swap_all(v):
    return lax.all_to_all(v, "seq", split_axis=0, concat_axis=0, tiled=True)


def shards(hidden, query_weight, key_memory, value_memory, block_len, nbr_block, out_grad):
    s = lax.axis_index("seq")
    m = lax.axis_index("mp")
    core = s % NC
    cx, cy = s // (NY * NC), (s // NC) % NY
    off = jnp.array(OFF, jnp.int32)
    chips = (((cx + off[None, :]) % NX) * NY + (cy + off[:, None]) % NY).reshape(-1).astype(jnp.int32)
    core1 = core.reshape(1).astype(jnp.int32)
    last = (s % 8 == 7).astype(jnp.int32).reshape(1)
    first = (s % 8 == 0).astype(jnp.int32).reshape(1)
    ahead = jnp.array((4, 3, -3, 2, -2, 1, -1, 0), jnp.int32)
    order = jnp.concatenate([(m + ahead) % NM, first]).astype(jnp.int32)
    mine = nbr_block.T

    pay, left, right, g_head = prepare(mine, block_len, key_memory, value_memory, query_weight, out_grad)
    g_next = to_seq(g_head, -1)
    weight = lax.all_gather(query_weight, "seq", axis=0, tiled=True)
    held = swap_all(pay)
    facts = held[:, 2 * QR, : NP + 2].astype(jnp.int32)
    sent = pick(facts, held).reshape(NS, NP * QR, HD)
    kv = swap_all(sent).reshape(2, NH, RQ, NP, QR, HD)
    queries = jnp.dot(hidden, weight, preferred_element_type=F32)
    n_own = to_seq(queries[:GROUP].astype(BF), -1).astype(F32)
    own = queries.astype(BF).astype(F32)
    q_other = jnp.zeros_like(own)
    n_sib = jnp.zeros_like(n_own)
    parts = (mine, facts, last, own, q_other, n_own, n_sib, out_grad, g_next, kv)
    att_end, gq_end, terms = attend((3,), *parts)
    gq_tail = to_seq(gq_end, 1)
    att_tail = to_seq(att_end, 1)
    att_al, gq_al, terms = attend((0, 1, 2), *parts, into=terms)
    got = swap_all(terms.reshape(NS, NP * QR, HD))

    gone = jnp.where(first[0] == 1, jnp.zeros((), BF), gq_tail[1:])
    qg = jnp.concatenate([gone, gq_al, gq_end[:1]], 0)
    run = lax.psum_scatter(
        lax.dot_general(qg, weight, (((1,), (1,)), ((), ())), preferred_element_type=F32).astype(BF),
        "mp", scatter_dimension=0, tiled=True)
    sums = total(facts, got.reshape(NS * NP, QR, HD)).reshape(NS, 2 * QR, HD)
    back = swap_all(sums)
    back = back.reshape(2, NH, RQ, 2, QR, HD)
    grads = back.transpose(0, 3, 2, 4, 1, 5).reshape(2, 2 * NLEN, FT)

    dead = jnp.where(first[0] == 1, jnp.zeros((), BF), att_tail[1:])
    attended = jnp.concatenate([dead, att_al, att_end[:1]], 0)
    return attended, run, grads[0], grads[1]


def solution(mesh):
    return jax.shard_map(
        shards,
        mesh=mesh,
        in_specs=(
            P("seq", None),
            P("seq", "mp"),
            P("seq", "mp"),
            P("seq", "mp"),
            P("seq"),
            P("seq", None),
            P("seq", "mp"),
        ),
        out_specs=(P("seq", "mp"), P(("seq", "mp"), None), P("seq", "mp"), P("seq", "mp")),
        check_vma=False,
    )
```

```python
import functools

import jax
import jax.numpy as jnp
from jax import lax
from jax.experimental import pallas as pl
from jax.experimental.pallas import tpu as pltpu
from jax.sharding import PartitionSpec as P

HD = 128
GROUP = 64
NLEN = 128
SEQ_LEN = 2048
RIM = GROUP - 1
NS = 32
TOK = 256
FT = 512
DM = 8192
NH = FT // HD
NP = 8
NB = 64
RQ = 4
QR = NLEN // RQ
BF = jnp.bfloat16
F32 = jnp.float32
NEG_FILL = -1e30
MIB = 1 << 20
WIDE = 60 * MIB


def to_seq(v, by):
    return lax.ppermute(v, "seq", [(i, (i + by) % NS) for i in range(NS)])


def prepare_kernel(mine, lens, key, value, pay):
    lane = lax.broadcasted_iota(jnp.int32, (16, HD), 1)
    meta = jnp.zeros((16, HD), jnp.int32)
    for i in range(NP):
        meta = jnp.where(lane == i, mine[i % 2, i // 2], meta)
    for i in range(2):
        meta = jnp.where(lane == NP + i, lens[i], meta)
    meta = meta.astype(F32).astype(BF)
    for which, ref in ((0, key), (1, value)):
        for h in range(NH):
            for r in range(RQ):
                j = (which * NH + h) * RQ + r
                for blk in range(2):
                    at = blk * NLEN + r * QR
                    pay[j, blk * QR : (blk + 1) * QR] = ref[at : at + QR, h * HD : (h + 1) * HD]
                pay[j, 2 * QR :] = meta


def prepare(mine, lens, key, value):
    smem = pl.BlockSpec(memory_space=pltpu.SMEM)

    def full(*shape):
        return pl.BlockSpec(shape, lambda i: (0,) * len(shape))

    return pl.pallas_call(
        prepare_kernel,
        grid=(1,),
        out_shape=jax.ShapeDtypeStruct((NS, 2 * QR + 16, HD), BF),
        in_specs=[smem, smem, full(256, FT), full(256, FT)],
        out_specs=full(NS, 2 * QR + 16, HD),
        compiler_params=pltpu.CompilerParams(vmem_limit_bytes=WIDE),
    )(mine, lens, key, value)


def pick_kernel(facts, held, out):
    count = out.shape[0] // NP
    base = pl.program_id(0) * count

    def step(i, _):
        for n in range(NP):
            b = facts[base + i, n]
            at = pl.multiple_of(jnp.bitwise_and(b, 1) * QR, QR)
            out[i * NP + n] = held[lax.shift_right_logical(b, 1), pl.ds(at, QR)]
        return 0

    lax.fori_loop(0, count, step, 0, unroll=2)


def pick(facts, held):
    count = NS * NP // 2
    return pl.pallas_call(
        pick_kernel,
        out_shape=jax.ShapeDtypeStruct((NS * NP, QR, HD), BF),
        grid=(2,),
        in_specs=[pl.BlockSpec(memory_space=pltpu.SMEM), pl.BlockSpec(held.shape, lambda i: (0, 0, 0))],
        out_specs=pl.BlockSpec((count, QR, HD), lambda i: (i, 0, 0)),
        compiler_params=pltpu.CompilerParams(vmem_limit_bytes=WIDE),
        cost_estimate=pl.CostEstimate(flops=0, bytes_accessed=1024, transcendentals=0),
    )(facts, held)


def total_kernel(facts, terms, out, acc):
    acc[...] = jnp.zeros_like(acc)

    def step(i, _):
        for n in range(NP):
            b = facts[i, n]
            acc[b] = acc[b] + terms[i * NP + n].astype(F32)
        return 0

    lax.fori_loop(0, NS, step, 0, unroll=2)
    out[...] = acc[...].astype(BF)


def total(facts, terms):
    return pl.pallas_call(
        total_kernel,
        out_shape=jax.ShapeDtypeStruct((NB, QR, HD), BF),
        in_specs=[pl.BlockSpec(memory_space=pltpu.SMEM), pl.BlockSpec(memory_space=pltpu.VMEM)],
        out_specs=pl.BlockSpec(memory_space=pltpu.VMEM),
        scratch_shapes=[pltpu.VMEM((NB, QR, HD), F32)],
        compiler_params=pltpu.CompilerParams(vmem_limit_bytes=16 * MIB),
    )(facts, terms)


def attend_kernel(groups, heads, seat, facts, q, g, kv, *rest):
    before, (att, gq, terms) = rest[:-3], rest[-3:]

    def mm(p, r, dims):
        return lax.dot_general(p, r, (dims, ((), ())), preferred_element_type=F32)

    scale = HD ** (-0.5)
    lane = lax.broadcasted_iota(jnp.int32, (GROUP, 2 * NLEN), 1)
    units = [(h, i) for h in range(heads) for i in range(len(groups))]
    count = range(len(units))
    valid = []
    for grp in groups:
        blk0, blk1 = facts[seat[0], 2 * grp], facts[seat[0], 2 * grp + 1]
        len0 = facts[lax.shift_right_logical(blk0, 1), NP + jnp.bitwise_and(blk0, 1)]
        len1 = facts[lax.shift_right_logical(blk1, 1), NP + jnp.bitwise_and(blk1, 1)]
        valid.append(lane < jnp.where(lane < NLEN, len0, len1 + NLEN))
    cols = [slice(h * HD, (h + 1) * HD) for h in range(heads)]
    rows = [slice(i * GROUP, (i + 1) * GROUP) for i in range(len(groups))]
    tok = [slice(grp * GROUP, (grp + 1) * GROUP) for grp in groups]

    def block(which, h, i):
        return jnp.concatenate([kv[which, h, r, 2 * groups[i] + n] for n in range(2) for r in range(RQ)], 0)

    qs = [q[tok[i], cols[h]] for h, i in units]
    gs = [g[tok[i], cols[h]] for h, i in units]
    keys = [block(0, h, i) for h, i in units]
    vals = [block(1, h, i) for h, i in units]
    scores = [mm(qs[u], keys[u], ((1,), (1,))) for u in count]
    grad_prob = [mm(gs[u], vals[u], ((1,), (1,))) for u in count]
    ex, inv = [], []
    for u in count:
        ok = valid[units[u][1]]
        masked = jnp.where(ok, scores[u] * scale, NEG_FILL)
        top = jnp.max(masked, axis=1, keepdims=True)
        e = jnp.where(ok, jnp.exp(masked - top), 0.0)
        ex.append(e)
        inv.append(1.0 / jnp.sum(e, axis=1, keepdims=True))
    outs = [(mm(ex[u].astype(BF), vals[u], ((1,), (0,))) * inv[u]).astype(BF) for u in count]
    prob = [ex[u] * inv[u] for u in count]
    vt = [mm(prob[u].astype(BF), gs[u], ((0,), (0,))).astype(BF) for u in count]
    ds = []
    for u in count:
        delta = jnp.sum(gs[u].astype(F32) * outs[u].astype(F32), axis=1, keepdims=True)
        ds.append((prob[u] * (grad_prob[u] - delta) * scale).astype(BF))
    gqs = [mm(ds[u], keys[u], ((1,), (0,))).astype(BF) for u in count]
    kt = [mm(ds[u], qs[u], ((0,), (0,))).astype(BF) for u in count]
    shift = 2 * groups[0] if before else 0
    if before:
        terms[:, :, :, :shift] = before[0][...]
    for u, (h, i) in enumerate(units):
        att[rows[i], cols[h]] = outs[u]
        gq[rows[i], cols[h]] = gqs[u]
        for n in range(2):
            for r in range(RQ):
                part = slice((n * RQ + r) * QR, (n * RQ + r + 1) * QR)
                terms[0, h, r, shift + 2 * i + n] = kt[u][part]
                terms[1, h, r, shift + 2 * i + n] = vt[u][part]


def attend(groups, heads, seat, facts, q, g, kv, before=None):
    count = len(groups) * GROUP
    pairs = 2 * len(groups) if before is None else NP
    tok = pl.BlockSpec((TOK, heads * HD), lambda h, *_: (0, h))
    out = pl.BlockSpec((count, heads * HD), lambda h, *_: (0, h))

    def mem(n):
        return pl.BlockSpec((2, heads, RQ, n, QR, HD), lambda h, *_: (0, h, 0, 0, 0, 0))

    rows = jax.ShapeDtypeStruct((count, FT), BF)
    read = NP if before is not None else 2
    specs, operands = [tok, tok, mem(read)], (q, g, kv)
    if before is not None:
        specs, operands = specs + [mem(before.shape[3])], operands + (before,)
    return pl.pallas_call(
        functools.partial(attend_kernel, groups, heads),
        out_shape=(rows, rows, jax.ShapeDtypeStruct((2, NH, RQ, pairs, QR, HD), BF)),
        grid_spec=pltpu.PrefetchScalarGridSpec(
            num_scalar_prefetch=2,
            grid=(NH // heads,),
            in_specs=specs,
            out_specs=(out, out, mem(pairs)),
        ),
        compiler_params=pltpu.CompilerParams(vmem_limit_bytes=32 * MIB),
        cost_estimate=pl.CostEstimate(
            flops=100_000_000 * len(groups), bytes_accessed=2 * MIB * len(groups), transcendentals=0
        ),
    )(seat, facts, *operands)


def swap_all(v):
    return lax.all_to_all(v, "seq", split_axis=0, concat_axis=0, tiled=True)


def shards(hidden, query_weight, key_memory, value_memory, block_len, nbr_block, out_grad):
    s = lax.axis_index("seq")
    starts = s % (SEQ_LEN // TOK) == 0
    seat = s.astype(jnp.int32).reshape(1)
    zero = jnp.zeros((), BF)

    weight = lax.all_gather(query_weight, "seq", axis=0, tiled=True)

    held = swap_all(prepare(nbr_block.T, block_len, key_memory, value_memory))
    facts = held[:, 2 * QR, : NP + 2].astype(jnp.int32)
    facts = jnp.concatenate([jnp.roll(facts[:, NP - 2 : NP], 1, axis=0), facts[:, : NP - 2], facts[:, NP:]], 1)
    sent = pick(facts, held).reshape(NS, NP * QR, HD)
    kv = swap_all(sent).reshape(2, NH, RQ, NP, QR, HD)

    h_prev, g_prev = to_seq(hidden[TOK - 1 :], 1), to_seq(out_grad[TOK - 1 :], 1)
    h_rows = jnp.concatenate([h_prev, hidden[: TOK - 1]], 0)
    g_rows = jnp.concatenate([g_prev, jnp.where(starts, zero, out_grad[:RIM]), out_grad[RIM : TOK - 1]], 0)
    queries = jnp.dot(h_rows, weight, preferred_element_type=F32).astype(BF)

    att_rim, gq_rim, terms = attend((0,), NH, seat, facts, queries, g_rows, kv)
    gq_last, att_last = to_seq(gq_rim[:1], -1), to_seq(att_rim[:1], -1)
    att, gq, terms = attend((1, 2, 3), 2, seat, facts, queries, g_rows, kv, terms)

    query_grad = jnp.concatenate([jnp.where(starts, zero, gq_rim[1:]), gq, gq_last], 0)
    run = lax.psum_scatter(
        lax.dot_general(
            query_grad, weight, (((1,), (1,)), ((), ())), preferred_element_type=F32
        ).astype(BF),
        "mp",
        scatter_dimension=0,
        tiled=True,
    )
    got = swap_all(terms.reshape(NS, NP * QR, HD))
    sums = total(facts, got.reshape(NS * NP, QR, HD)).reshape(NS, 2 * QR, HD)
    back = swap_all(sums).reshape(2, NH, RQ, 2, QR, HD)
    grads = back.transpose(0, 3, 2, 4, 1, 5).reshape(2, 2 * NLEN, FT)

    attended = jnp.concatenate([jnp.where(starts, zero, att_rim[1:]), att, att_last], 0)
    return attended, run, grads[0], grads[1]


def solution(mesh):
    return jax.shard_map(
        shards,
        mesh=mesh,
        in_specs=(
            P("seq", None),
            P("seq", "mp"),
            P("seq", "mp"),
            P("seq", "mp"),
            P("seq"),
            P("seq", None),
            P("seq", "mp"),
        ),
        out_specs=(P("seq", "mp"), P(("seq", "mp"), None), P("seq", "mp"), P("seq", "mp")),
        check_vma=False,
    )
```

```python
import jax
import jax.numpy as jnp
from jax import lax
from jax.experimental import pallas as pl
from jax.experimental.pallas import tpu as pltpu
from jax.sharding import PartitionSpec as P

HD = 128
GROUP = 64
NLEN = 128
SEQ_LEN = 2048
RIM = GROUP - 1
NS = 32
NM = 8
TOK = 256
FT = 512
DM = 8192
NH = FT // HD
NP = 8
NB = 64
RQ = 4
QR = NLEN // RQ
BF = jnp.bfloat16
F32 = jnp.float32
NEG_FILL = -1e30
MIB = 1 << 20
WIDE = 60 * MIB


def to_seq(v, by):
    return lax.ppermute(v, "seq", [(i, (i + by) % NS) for i in range(NS)])


def prepare_kernel(mine, lens, key, value, pay):
    lane = lax.broadcasted_iota(jnp.int32, (16, HD), 1)
    meta = jnp.zeros((16, HD), jnp.int32)
    for i in range(NP):
        meta = jnp.where(lane == i, mine[i % 2, i // 2], meta)
    for i in range(2):
        meta = jnp.where(lane == NP + i, lens[i], meta)
    meta = meta.astype(F32).astype(BF)
    for which, ref in ((0, key), (1, value)):
        for h in range(NH):
            for r in range(RQ):
                j = (which * NH + h) * RQ + r
                for blk in range(2):
                    at = blk * NLEN + r * QR
                    pay[j, blk * QR : (blk + 1) * QR] = ref[at : at + QR, h * HD : (h + 1) * HD]
                pay[j, 2 * QR :] = meta


def prepare(mine, lens, key, value):
    smem = pl.BlockSpec(memory_space=pltpu.SMEM)

    def full(*shape):
        return pl.BlockSpec(shape, lambda i: (0,) * len(shape))

    return pl.pallas_call(
        prepare_kernel,
        grid=(1,),
        out_shape=jax.ShapeDtypeStruct((NS, 2 * QR + 16, HD), BF),
        in_specs=[smem, smem, full(256, FT), full(256, FT)],
        out_specs=full(NS, 2 * QR + 16, HD),
        compiler_params=pltpu.CompilerParams(vmem_limit_bytes=WIDE),
    )(mine, lens, key, value)


def pick_kernel(facts, held, out):
    count = out.shape[0] // NP
    base = pl.program_id(0) * count

    def step(i, _):
        for n in range(NP):
            b = facts[base + i, n]
            at = pl.multiple_of(jnp.bitwise_and(b, 1) * QR, QR)
            out[i * NP + n] = held[lax.shift_right_logical(b, 1), pl.ds(at, QR)]
        return 0

    lax.fori_loop(0, count, step, 0, unroll=2)


def pick(facts, held):
    count = NS * NP // 2
    return pl.pallas_call(
        pick_kernel,
        out_shape=jax.ShapeDtypeStruct((NS * NP, QR, HD), BF),
        grid=(2,),
        in_specs=[pl.BlockSpec(memory_space=pltpu.SMEM), pl.BlockSpec(held.shape, lambda i: (0, 0, 0))],
        out_specs=pl.BlockSpec((count, QR, HD), lambda i: (i, 0, 0)),
        compiler_params=pltpu.CompilerParams(vmem_limit_bytes=WIDE),
        cost_estimate=pl.CostEstimate(flops=0, bytes_accessed=1024, transcendentals=0),
    )(facts, held)


def total_kernel(facts, terms, out, acc):
    acc[...] = jnp.zeros_like(acc)

    def step(i, _):
        for n in range(NP):
            b = facts[i, n]
            acc[b] = acc[b] + terms[i * NP + n].astype(F32)
        return 0

    lax.fori_loop(0, NS, step, 0, unroll=2)
    out[...] = acc[...].astype(BF)


def total(facts, terms):
    return pl.pallas_call(
        total_kernel,
        out_shape=jax.ShapeDtypeStruct((NB, QR, HD), BF),
        in_specs=[pl.BlockSpec(memory_space=pltpu.SMEM), pl.BlockSpec(memory_space=pltpu.VMEM)],
        out_specs=pl.BlockSpec(memory_space=pltpu.VMEM),
        scratch_shapes=[pltpu.VMEM((NB, QR, HD), F32)],
        compiler_params=pltpu.CompilerParams(vmem_limit_bytes=16 * MIB),
    )(facts, terms)


def mm(p, r, dims):
    return lax.dot_general(p, r, (dims, ((), ())), preferred_element_type=F32)


def attend_units(units, seat, facts, q, g, kv, att, gq, terms, first):
    scale = HD ** (-0.5)
    lane = lax.broadcasted_iota(jnp.int32, (GROUP, 2 * NLEN), 1)
    count = range(len(units))
    valid = {}
    for grp in sorted({grp for _, grp in units}):
        blk0, blk1 = facts[seat[0], 2 * grp], facts[seat[0], 2 * grp + 1]
        len0 = facts[lax.shift_right_logical(blk0, 1), NP + jnp.bitwise_and(blk0, 1)]
        len1 = facts[lax.shift_right_logical(blk1, 1), NP + jnp.bitwise_and(blk1, 1)]
        valid[grp] = lane < jnp.where(lane < NLEN, len0, len1 + NLEN)

    def cols(h):
        return slice(h * HD, (h + 1) * HD)

    def rows(grp):
        return slice(grp * GROUP, (grp + 1) * GROUP)

    def block(which, h, grp):
        return jnp.concatenate([kv[which, h, r, 2 * grp + n] for n in range(2) for r in range(RQ)], 0)

    qs = [q[rows(grp), cols(h)] for h, grp in units]
    gs = [g[rows(grp), cols(h)] for h, grp in units]
    keys = [block(0, h, grp) for h, grp in units]
    vals = [block(1, h, grp) for h, grp in units]
    scores = [mm(qs[u], keys[u], ((1,), (1,))) for u in count]
    grad_prob = [mm(gs[u], vals[u], ((1,), (1,))) for u in count]
    ex, inv = [], []
    for u in count:
        ok = valid[units[u][1]]
        masked = jnp.where(ok, scores[u] * scale, NEG_FILL)
        top = jnp.max(masked, axis=1, keepdims=True)
        e = jnp.where(ok, jnp.exp(masked - top), 0.0)
        ex.append(e)
        inv.append(1.0 / jnp.sum(e, axis=1, keepdims=True))
    outs = [(mm(ex[u].astype(BF), vals[u], ((1,), (0,))) * inv[u]).astype(BF) for u in count]
    prob = [ex[u] * inv[u] for u in count]
    vt = [mm(prob[u].astype(BF), gs[u], ((0,), (0,))).astype(BF) for u in count]
    ds = []
    for u in count:
        delta = jnp.sum(gs[u].astype(F32) * outs[u].astype(F32), axis=1, keepdims=True)
        ds.append((prob[u] * (grad_prob[u] - delta) * scale).astype(BF))
    gqs = [mm(ds[u], keys[u], ((1,), (0,))).astype(BF) for u in count]
    kt = [mm(ds[u], qs[u], ((0,), (0,))).astype(BF) for u in count]
    for u, (h, grp) in enumerate(units):
        att[rows(grp - first), cols(h)] = outs[u]
        gq[rows(grp - first), cols(h)] = gqs[u]
        for n in range(2):
            for r in range(RQ):
                part = slice((n * RQ + r) * QR, (n * RQ + r + 1) * QR)
                terms[0, h, r, 2 * grp + n] = kt[u][part]
                terms[1, h, r, 2 * grp + n] = vt[u][part]


def core_kernel(seat, facts, g, h, w, kv, att, whole, out, q, gq, terms, hbuf, wbuf, kvbuf, buf, in_sems, out_sems, sems):
    parts = wbuf.shape[0]
    size = DM // parts

    def loads(i):
        at = pl.ds(i * size, size)
        return (
            pltpu.make_async_copy(w.at[at], wbuf.at[i], in_sems.at[0, i]),
            pltpu.make_async_copy(h.at[:, at], hbuf.at[i], in_sems.at[1, i]),
        )

    def store(i):
        return pltpu.make_async_copy(buf.at[i], out.at[:, pl.ds(i * size, size)], out_sems.at[i])

    for i in range(parts):
        for cp in loads(i):
            cp.start()
    blocks = pltpu.make_async_copy(kv, kvbuf, sems.at[0])
    blocks.start()
    acc = None
    for i in range(parts):
        for cp in loads(i):
            cp.wait()
        term = jnp.dot(hbuf[i], wbuf[i], preferred_element_type=F32)
        acc = term if acc is None else acc + term
    q[...] = acc.astype(BF)
    blocks.wait()
    for half in range(2):
        units = [(head, grp) for head in (2 * half, 2 * half + 1) for grp in range(TOK // GROUP)]
        attend_units(units, seat, facts, q, g, kvbuf, att, gq, terms, 0)
    keep = pltpu.make_async_copy(terms, whole, sems.at[1])
    keep.start()
    for i in range(parts):
        buf[i] = mm(gq[...], wbuf[i], ((1,), (1,))).astype(BF)
        store(i).start()
    for i in range(parts):
        store(i).wait()
    keep.wait()


def attend(seat, facts, g, h, weight, kv, parts=8):
    def full(*shape):
        return pl.BlockSpec(shape, lambda i, *_: (0,) * len(shape))

    anywhere = pl.BlockSpec(memory_space=pl.ANY)
    whole = (2, NH, RQ, NP, QR, HD)
    rows = jax.ShapeDtypeStruct((TOK, FT), BF)
    return pl.pallas_call(
        core_kernel,
        out_shape=(rows, jax.ShapeDtypeStruct(whole, BF), jax.ShapeDtypeStruct((TOK, DM), BF)),
        grid_spec=pltpu.PrefetchScalarGridSpec(
            num_scalar_prefetch=2,
            grid=(1,),
            in_specs=[full(TOK, FT), anywhere, anywhere, anywhere],
            out_specs=(full(TOK, FT), anywhere, anywhere),
            scratch_shapes=[
                pltpu.VMEM((TOK, FT), BF),
                pltpu.VMEM((TOK, FT), BF),
                pltpu.VMEM(whole, BF),
                pltpu.VMEM((parts, TOK, DM // parts), BF),
                pltpu.VMEM((parts, DM // parts, FT), BF),
                pltpu.VMEM(whole, BF),
                pltpu.VMEM((parts, TOK, DM // parts), BF),
                pltpu.SemaphoreType.DMA((2, parts)),
                pltpu.SemaphoreType.DMA((parts,)),
                pltpu.SemaphoreType.DMA((2,)),
            ],
        ),
        compiler_params=pltpu.CompilerParams(vmem_limit_bytes=50 * MIB),
        cost_estimate=pl.CostEstimate(flops=4 * TOK * DM * FT, bytes_accessed=20 * MIB, transcendentals=0),
    )(seat, facts, g, h, weight, kv)


def swap_all(v):
    return lax.all_to_all(v, "seq", split_axis=0, concat_axis=0, tiled=True)


def shards(hidden, query_weight, key_memory, value_memory, block_len, nbr_block, out_grad):
    s = lax.axis_index("seq")
    starts = s % (SEQ_LEN // TOK) == 0
    seat = s.astype(jnp.int32).reshape(1)
    zero = jnp.zeros((), BF)

    pay = prepare(nbr_block.T, block_len, key_memory, value_memory)
    pay, query_weight = lax.optimization_barrier((pay, query_weight))
    weight = lax.all_gather(query_weight, "seq", axis=0, tiled=True)
    held = swap_all(pay)
    facts = held[:, 2 * QR, : NP + 2].astype(jnp.int32)
    facts = jnp.concatenate([jnp.roll(facts[:, NP - 2 : NP], 1, axis=0), facts[:, : NP - 2], facts[:, NP:]], 1)
    sent = pick(facts, held).reshape(NS, NP * QR, HD)
    kv = swap_all(sent).reshape(2, NH, RQ, NP, QR, HD)

    h_prev, g_prev = to_seq(hidden[TOK - 1 :], 1), to_seq(out_grad[TOK - 1 :], 1)
    h_rows = jnp.concatenate([h_prev, hidden[: TOK - 1]], 0)
    g_rows = jnp.concatenate([g_prev, jnp.where(starts, zero, out_grad[:RIM]), out_grad[RIM : TOK - 1]], 0)
    att, terms, partial = attend(seat, facts, g_rows, h_rows, weight, kv)
    att_last = to_seq(att[:1], -1)
    run = lax.psum_scatter(partial, "mp", scatter_dimension=0, tiled=True)
    count = NS * NM
    run_last = lax.ppermute(run[:1], ("seq", "mp"), [(i, (i - 1) % count) for i in range(count)])
    run = jnp.concatenate([run[1:], run_last], 0)
    got = swap_all(terms.reshape(NS, NP * QR, HD))
    sums = total(facts, got.reshape(NS * NP, QR, HD)).reshape(NS, 2 * QR, HD)
    back = swap_all(sums).reshape(2, NH, RQ, 2, QR, HD)
    grads = back.transpose(0, 3, 2, 4, 1, 5).reshape(2, 2 * NLEN, FT)

    attended = jnp.concatenate([jnp.where(starts, zero, att[1:GROUP]), att[GROUP:], att_last], 0)
    return attended, run, grads[0], grads[1]


def solution(mesh):
    return jax.shard_map(
        shards,
        mesh=mesh,
        in_specs=(
            P("seq", None),
            P("seq", "mp"),
            P("seq", "mp"),
            P("seq", "mp"),
            P("seq"),
            P("seq", None),
            P("seq", "mp"),
        ),
        out_specs=(P("seq", "mp"), P(("seq", "mp"), None), P("seq", "mp"), P("seq", "mp")),
        check_vma=False,
    )
```

```python
import jax
import jax.numpy as jnp
from jax import lax
from jax.experimental import pallas as pl
from jax.experimental.pallas import tpu as pltpu
from jax.sharding import PartitionSpec as P

HD = 128
GROUP = 64
NLEN = 128
SEQ_LEN = 2048
RIM = GROUP - 1
NS = 32
NM = 8
TOK = 256
FT = 512
DM = 8192
NH = FT // HD
NP = 8
NB = 64
RQ = 4
QR = NLEN // RQ
BF = jnp.bfloat16
F32 = jnp.float32
NEG_FILL = -1e30
MIB = 1 << 20
WIDE = 60 * MIB


def to_seq(v, by):
    return lax.ppermute(v, "seq", [(i, (i + by) % NS) for i in range(NS)])


def prepare_kernel(mine, lens, key, value, pay):
    lane = lax.broadcasted_iota(jnp.int32, (16, HD), 1)
    meta = jnp.zeros((16, HD), jnp.int32)
    for i in range(NP):
        meta = jnp.where(lane == i, mine[i % 2, i // 2], meta)
    for i in range(2):
        meta = jnp.where(lane == NP + i, lens[i], meta)
    meta = meta.astype(F32).astype(BF)
    for which, ref in ((0, key), (1, value)):
        for h in range(NH):
            for r in range(RQ):
                j = (which * NH + h) * RQ + r
                for blk in range(2):
                    at = blk * NLEN + r * QR
                    pay[j, blk * QR : (blk + 1) * QR] = ref[at : at + QR, h * HD : (h + 1) * HD]
                pay[j, 2 * QR :] = meta


def prepare(mine, lens, key, value):
    smem = pl.BlockSpec(memory_space=pltpu.SMEM)

    def full(*shape):
        return pl.BlockSpec(shape, lambda i: (0,) * len(shape))

    return pl.pallas_call(
        prepare_kernel,
        grid=(1,),
        out_shape=jax.ShapeDtypeStruct((NS, 2 * QR + 16, HD), BF),
        in_specs=[smem, smem, full(256, FT), full(256, FT)],
        out_specs=full(NS, 2 * QR + 16, HD),
        compiler_params=pltpu.CompilerParams(vmem_limit_bytes=WIDE),
    )(mine, lens, key, value)


def pick_kernel(facts, held, out):
    count = out.shape[0] // NP
    base = pl.program_id(0) * count

    def step(i, _):
        for n in range(NP):
            b = facts[base + i, n]
            at = pl.multiple_of(jnp.bitwise_and(b, 1) * QR, QR)
            out[i * NP + n] = held[lax.shift_right_logical(b, 1), pl.ds(at, QR)]
        return 0

    lax.fori_loop(0, count, step, 0, unroll=2)


def pick(facts, held):
    count = NS * NP // 2
    return pl.pallas_call(
        pick_kernel,
        out_shape=jax.ShapeDtypeStruct((NS * NP, QR, HD), BF),
        grid=(2,),
        in_specs=[pl.BlockSpec(memory_space=pltpu.SMEM), pl.BlockSpec(held.shape, lambda i: (0, 0, 0))],
        out_specs=pl.BlockSpec((count, QR, HD), lambda i: (i, 0, 0)),
        compiler_params=pltpu.CompilerParams(vmem_limit_bytes=WIDE),
        cost_estimate=pl.CostEstimate(flops=0, bytes_accessed=1024, transcendentals=0),
    )(facts, held)


def total_kernel(facts, terms, out, acc):
    acc[...] = jnp.zeros_like(acc)

    def step(i, _):
        for n in range(NP):
            b = facts[i, n]
            acc[b] = acc[b] + terms[i * NP + n].astype(F32)
        return 0

    lax.fori_loop(0, NS, step, 0, unroll=2)
    out[...] = acc[...].astype(BF)


def total(facts, terms):
    return pl.pallas_call(
        total_kernel,
        out_shape=jax.ShapeDtypeStruct((NB, QR, HD), BF),
        in_specs=[pl.BlockSpec(memory_space=pltpu.SMEM), pl.BlockSpec(memory_space=pltpu.VMEM)],
        out_specs=pl.BlockSpec(memory_space=pltpu.VMEM),
        scratch_shapes=[pltpu.VMEM((NB, QR, HD), F32)],
        compiler_params=pltpu.CompilerParams(vmem_limit_bytes=16 * MIB),
    )(facts, terms)


def mm(p, r, dims):
    return lax.dot_general(p, r, (dims, ((), ())), preferred_element_type=F32)


def attend_units(units, seat, facts, q, g, kv, att, gq, terms, first):
    scale = HD ** (-0.5)
    lane = lax.broadcasted_iota(jnp.int32, (GROUP, 2 * NLEN), 1)
    count = range(len(units))
    valid = {}
    for grp in sorted({grp for _, grp in units}):
        blk0, blk1 = facts[seat[0], 2 * grp], facts[seat[0], 2 * grp + 1]
        len0 = facts[lax.shift_right_logical(blk0, 1), NP + jnp.bitwise_and(blk0, 1)]
        len1 = facts[lax.shift_right_logical(blk1, 1), NP + jnp.bitwise_and(blk1, 1)]
        valid[grp] = lane < jnp.where(lane < NLEN, len0, len1 + NLEN)

    def cols(h):
        return slice(h * HD, (h + 1) * HD)

    def rows(grp):
        return slice(grp * GROUP, (grp + 1) * GROUP)

    def block(which, h, grp):
        return jnp.concatenate([kv[which, h, r, 2 * grp + n] for n in range(2) for r in range(RQ)], 0)

    qs = [q[rows(grp), cols(h)] for h, grp in units]
    gs = [g[rows(grp), cols(h)] for h, grp in units]
    keys = [block(0, h, grp) for h, grp in units]
    vals = [block(1, h, grp) for h, grp in units]
    scores = [mm(qs[u], keys[u], ((1,), (1,))) for u in count]
    grad_prob = [mm(gs[u], vals[u], ((1,), (1,))) for u in count]
    ex, inv = [], []
    for u in count:
        ok = valid[units[u][1]]
        masked = jnp.where(ok, scores[u] * scale, NEG_FILL)
        top = jnp.max(masked, axis=1, keepdims=True)
        e = jnp.where(ok, jnp.exp(masked - top), 0.0)
        ex.append(e)
        inv.append(1.0 / jnp.sum(e, axis=1, keepdims=True))
    outs = [(mm(ex[u].astype(BF), vals[u], ((1,), (0,))) * inv[u]).astype(BF) for u in count]
    prob = [ex[u] * inv[u] for u in count]
    vt = [mm(prob[u].astype(BF), gs[u], ((0,), (0,))).astype(BF) for u in count]
    ds = []
    for u in count:
        delta = jnp.sum(gs[u].astype(F32) * outs[u].astype(F32), axis=1, keepdims=True)
        ds.append((prob[u] * (grad_prob[u] - delta) * scale).astype(BF))
    gqs = [mm(ds[u], keys[u], ((1,), (0,))).astype(BF) for u in count]
    kt = [mm(ds[u], qs[u], ((0,), (0,))).astype(BF) for u in count]
    for u, (h, grp) in enumerate(units):
        att[rows(grp - first), cols(h)] = outs[u]
        gq[rows(grp - first), cols(h)] = gqs[u]
        for n in range(2):
            for r in range(RQ):
                part = slice((n * RQ + r) * QR, (n * RQ + r + 1) * QR)
                terms[0, h, r, 2 * grp + n] = kt[u][part]
                terms[1, h, r, 2 * grp + n] = vt[u][part]


def core_kernel(seat, facts, g, h, w, kv, att, whole, out, q, gq, terms, hbuf, wbuf, kvbuf, buf, in_sems, out_sems, sems):
    parts = wbuf.shape[0]
    size = DM // parts

    def loads(i):
        at = pl.ds(i * size, size)
        return (
            pltpu.make_async_copy(w.at[at], wbuf.at[i], in_sems.at[0, i]),
            pltpu.make_async_copy(h.at[:, at], hbuf.at[i], in_sems.at[1, i]),
        )

    def store(i):
        return pltpu.make_async_copy(buf.at[i], out.at[:, pl.ds(i * size, size)], out_sems.at[i])

    for i in range(parts):
        for cp in loads(i):
            cp.start()
    blocks = pltpu.make_async_copy(kv, kvbuf, sems.at[0])
    blocks.start()
    acc = None
    for i in range(parts):
        for cp in loads(i):
            cp.wait()
        term = jnp.dot(hbuf[i], wbuf[i], preferred_element_type=F32)
        acc = term if acc is None else acc + term
    q[...] = acc.astype(BF)
    blocks.wait()
    units = [(head, grp) for head in range(NH) for grp in range(TOK // GROUP)]
    attend_units(units, seat, facts, q, g, kvbuf, att, gq, terms, 0)
    keep = pltpu.make_async_copy(terms, whole, sems.at[1])
    keep.start()
    for i in range(parts):
        buf[i] = mm(gq[...], wbuf[i], ((1,), (1,))).astype(BF)
        store(i).start()
    for i in range(parts):
        store(i).wait()
    keep.wait()


def attend(seat, facts, g, h, weight, kv, parts=8):
    def full(*shape):
        return pl.BlockSpec(shape, lambda i, *_: (0,) * len(shape))

    anywhere = pl.BlockSpec(memory_space=pl.ANY)
    whole = (2, NH, RQ, NP, QR, HD)
    rows = jax.ShapeDtypeStruct((TOK, FT), BF)
    return pl.pallas_call(
        core_kernel,
        out_shape=(rows, jax.ShapeDtypeStruct(whole, BF), jax.ShapeDtypeStruct((TOK, DM), BF)),
        grid_spec=pltpu.PrefetchScalarGridSpec(
            num_scalar_prefetch=2,
            grid=(1,),
            in_specs=[full(TOK, FT), anywhere, anywhere, anywhere],
            out_specs=(full(TOK, FT), anywhere, anywhere),
            scratch_shapes=[
                pltpu.VMEM((TOK, FT), BF),
                pltpu.VMEM((TOK, FT), BF),
                pltpu.VMEM(whole, BF),
                pltpu.VMEM((parts, TOK, DM // parts), BF),
                pltpu.VMEM((parts, DM // parts, FT), BF),
                pltpu.VMEM(whole, BF),
                pltpu.VMEM((parts, TOK, DM // parts), BF),
                pltpu.SemaphoreType.DMA((2, parts)),
                pltpu.SemaphoreType.DMA((parts,)),
                pltpu.SemaphoreType.DMA((2,)),
            ],
        ),
        compiler_params=pltpu.CompilerParams(vmem_limit_bytes=50 * MIB),
        cost_estimate=pl.CostEstimate(flops=4 * TOK * DM * FT, bytes_accessed=20 * MIB, transcendentals=0),
    )(seat, facts, g, h, weight, kv)


def swap_all(v):
    return lax.all_to_all(v, "seq", split_axis=0, concat_axis=0, tiled=True)


def shards(hidden, query_weight, key_memory, value_memory, block_len, nbr_block, out_grad):
    s = lax.axis_index("seq")
    starts = s % (SEQ_LEN // TOK) == 0
    seat = s.astype(jnp.int32).reshape(1)
    zero = jnp.zeros((), BF)

    pay = prepare(nbr_block.T, block_len, key_memory, value_memory)
    pay, query_weight = lax.optimization_barrier((pay, query_weight))
    weight = lax.all_gather(query_weight, "seq", axis=0, tiled=True)
    held = swap_all(pay)
    facts = held[:, 2 * QR, : NP + 2].astype(jnp.int32)
    facts = jnp.concatenate([jnp.roll(facts[:, NP - 2 : NP], 1, axis=0), facts[:, : NP - 2], facts[:, NP:]], 1)
    sent = pick(facts, held).reshape(NS, NP * QR, HD)
    kv = swap_all(sent).reshape(2, NH, RQ, NP, QR, HD)

    h_prev, g_prev = to_seq(hidden[TOK - 1 :], 1), to_seq(out_grad[TOK - 1 :], 1)
    h_rows = jnp.concatenate([h_prev, hidden[: TOK - 1]], 0)
    g_rows = jnp.concatenate([g_prev, jnp.where(starts, zero, out_grad[:RIM]), out_grad[RIM : TOK - 1]], 0)
    att, terms, partial = attend(seat, facts, g_rows, h_rows, weight, kv)
    att_last = to_seq(att[:1], -1)
    run = lax.psum_scatter(partial, "mp", scatter_dimension=0, tiled=True)
    count = NS * NM
    run_last = lax.ppermute(run[:1], ("seq", "mp"), [(i, (i - 1) % count) for i in range(count)])
    run = jnp.concatenate([run[1:], run_last], 0)
    got = swap_all(terms.reshape(NS, NP * QR, HD))
    sums = total(facts, got.reshape(NS * NP, QR, HD)).reshape(NS, 2 * QR, HD)
    back = swap_all(sums).reshape(2, NH, RQ, 2, QR, HD)
    grads = back.transpose(0, 3, 2, 4, 1, 5).reshape(2, 2 * NLEN, FT)

    attended = jnp.concatenate([jnp.where(starts, zero, att[1:GROUP]), att[GROUP:], att_last], 0)
    return attended, run, grads[0], grads[1]


def solution(mesh):
    return jax.shard_map(
        shards,
        mesh=mesh,
        in_specs=(
            P("seq", None),
            P("seq", "mp"),
            P("seq", "mp"),
            P("seq", "mp"),
            P("seq"),
            P("seq", None),
            P("seq", "mp"),
        ),
        out_specs=(P("seq", "mp"), P(("seq", "mp"), None), P("seq", "mp"), P("seq", "mp")),
        check_vma=False,
    )
```
